256 devices in a mesh: gx: 8 (over z), gy: 16 (over x, y), gz: 2 (over core).
Axes of the slice: x: 4, y: 4, z: 8, core: 2. Of those that a mesh axis runs over, the one named last changes fastest.
Arguments:
- features: bfloat16 [64, 2097152], P(None, ('gx', 'gy', 'gz')), may hold values from -6 to 6
- grad_out: bfloat16 [64, 2097152], P(None, ('gx', 'gy', 'gz')), may hold values from -6 to 6
- weights: bfloat16 [27, 64, 64], replicated, may hold values from -0.15625 to 0.15625
- neighbor_map: int32 [27, 2097152], P(None, ('gx', 'gy', 'gz')), may hold values from 0 to 13824, as said below
- send_list: int32 [1441792], P(('gx', 'gy', 'gz')), may hold values from 0 to 8192, as said below
Outputs:
- grad_in: bfloat16 [64, 2097152], P(None, ('gx', 'gy', 'gz'))
- grad_weights: float32 [27, 64, 64], replicated
The draws below stay inside these ranges and needn't reach their ends.
Inputs may be any that keep to these rules, and one draw needn't show every extreme that they name: `neighbor_map`: for each offset and slot: a value below 8192 is a slot of the same block, 8192 to 13823 a column of the block's halo table, 13824 none. The middle offset 27 // 2 maps every used slot to itself; unused slots map to none at every offset. `send_list`: each entry is a used voxel slot of the sending block, or 8192 for an empty entry; at least half of every direction's entries are used, and one owner fills all of them.
All inputs are finite; a program needn't handle non-finite values.
Results may differ from the reference program's by a relative error of at most 0.001.
Values may be sent and summed in bfloat16 or wider, within the bound.
A program may use at most 64 MiB of HBM per device.

```python
import math
import jax
import jax.numpy as jnp
import numpy as np
from jax import lax

C = 64
KVOL = 27
VOX_DEV = 8192
FACE_CAP = 512
EDGE_CAP = 128
CORNER_CAP = 128
HALO = 5632
VOXELS = 2097152
N_GX = 8
N_GY = 16
N_GZ = 2
DEVICES = 256


def directions_drawn():
    found_list = []
    for kernel_weight in (1, 2, 3):
        for step_x in (-1, 0, 1):
            for step_y in (-1, 0, 1):
                for depth_step in (-1, 0, 1):
                    if abs(step_x) + abs(step_y) + abs(depth_step) == kernel_weight:
                        found_list.append((step_x, step_y, depth_step))
    return found_list


def drawn_room_limits():
    result_list = []
    for stencil_displacement in directions_drawn():
        nonzero = abs(stencil_displacement[0]) + abs(stencil_displacement[1]) + abs(stencil_displacement[2])
        if nonzero == 1:
            result_list.append(FACE_CAP)
        elif nonzero == 2:
            result_list.append(EDGE_CAP)
        else:
            result_list.append(CORNER_CAP)
    return result_list


def live_counts(key):
    counts = jax.random.randint(jax.random.fold_in(key, 7), (DEVICES,), VOX_DEV // 4, VOX_DEV + 1)
    counts = counts.at[0].set(VOX_DEV).at[1].set(VOX_DEV // 4)
    return counts.astype(jnp.int32)


def draw_neighbor_map(key, part):
    live_rows = live_counts(key)[None, :, None]
    shape_all = (KVOL, DEVICES, VOX_DEV)
    base_key = jax.random.fold_in(key, 23)
    local_pick = jax.random.randint(jax.random.fold_in(base_key, 1), shape_all, 0, VOX_DEV) % live_rows
    remote = VOX_DEV + jax.random.randint(jax.random.fold_in(base_key, 2), shape_all, 0, HALO)
    draw_kind = jax.random.randint(jax.random.fold_in(base_key, 3), shape_all, 0, 100)
    missing = VOX_DEV + HALO
    chosen = jnp.where(draw_kind < 45, local_pick, jnp.where(draw_kind < 55, remote, missing))
    slot_ids = jnp.arange(VOX_DEV, dtype=jnp.int32)[None, None, :] + 0 * chosen
    middle = (jnp.arange(KVOL) == KVOL // 2)[:, None, None]
    chosen = jnp.where(middle, slot_ids, chosen)
    chosen = jnp.where(slot_ids < live_rows, chosen, missing)
    return chosen.reshape(KVOL, DEVICES * VOX_DEV).astype(jnp.int32)


def draw_send_list(key, part):
    extent_host_array = np.array(drawn_room_limits(), dtype=np.int32)
    block_ids = np.repeat(np.arange(26), extent_host_array)
    position_np = np.concatenate([np.arange(width_one) for width_one in extent_host_array])
    base_key = jax.random.fold_in(key, 41)
    lowest = jnp.asarray(extent_host_array // 2)
    occupied_count = jax.random.randint(jax.random.fold_in(base_key, 1), (DEVICES, 26), 0, 1 << 20) % (lowest + 1)[None, :] + lowest[None, :]
    occupied_count = occupied_count.at[0].set(jnp.asarray(extent_host_array)).at[1, 0].set(lowest[0])
    per_slot = occupied_count[:, block_ids]
    live_rows = live_counts(key)[:, None]
    picks = jax.random.randint(jax.random.fold_in(base_key, 2), (DEVICES, HALO), 0, VOX_DEV) % live_rows
    result = jnp.where(jnp.asarray(position_np)[None, :] < per_slot, picks, VOX_DEV)
    result = result.at[0, 0].set(0)
    return result.reshape(DEVICES * HALO).astype(jnp.int32)


def levels(rng, dims, split, low, largest):
    def one(dim, shards_of):
        steps = jax.random.uniform(jax.random.fold_in(jax.random.fold_in(rng, 6), dim), (shards_of,), jnp.float32, low / len(split), largest / len(split))
        return jnp.repeat(jnp.exp(steps), dims[dim] // shards_of).reshape((-1,) + (1,) * (len(dims) - dim - 1))

    factor_of = one(*split[0])
    for cut in split[1:]:
        factor_of = factor_of * one(*cut)
    return factor_of


def noise(rng, extent, scale, reach, cuts=(), held_as=jnp.bfloat16):
    values = scale * jax.random.normal(rng, extent, jnp.float32)
    if cuts:
        values = values * levels(rng, extent, cuts, -0.22, 0.18)
    return jnp.clip(values, -reach, reach).astype(held_as)


def setup_inputs(seed: int = 0) -> dict:
    key_list = jax.random.split(jax.random.key(seed), 6)
    return {
        "features": noise(key_list[0], (C, VOXELS), 1.0, 6.0, ((1, 256),)),
        "grad_out": noise(key_list[1], (C, VOXELS), 1.0, 6.0, ((1, 256),)),
        "weights": noise(key_list[2], (KVOL, C, C), (KVOL * C) ** -0.5, 0.15625),
        "neighbor_map": draw_neighbor_map(jax.random.fold_in(key_list[5], 71), 0),
        "send_list": draw_send_list(jax.random.fold_in(key_list[5], 71), 0),
    }


def transfer_headings():
    found_list = []
    for kernel_weight in (1, 2, 3):
        for step_x in (-1, 0, 1):
            for step_y in (-1, 0, 1):
                for depth_step in (-1, 0, 1):
                    if abs(step_x) + abs(step_y) + abs(depth_step) == kernel_weight:
                        found_list.append((step_x, step_y, depth_step))
    return found_list

def block_room_limits():
    result_list = []
    for stencil_displacement in transfer_headings():
        nonzero = abs(stencil_displacement[0]) + abs(stencil_displacement[1]) + abs(stencil_displacement[2])
        if nonzero == 1:
            result_list.append(FACE_CAP)
        elif nonzero == 2:
            result_list.append(EDGE_CAP)
        else:
            result_list.append(CORNER_CAP)
    return result_list

def shifted(block, axis_pos, amount):
    length = block.shape[axis_pos]
    zero_slab = jnp.zeros_like(lax.slice_in_dim(block, 0, 1, axis=axis_pos))
    if amount == 1:
        return jnp.concatenate([zero_slab, lax.slice_in_dim(block, 0, length - 1, axis=axis_pos)], axis_pos)
    return jnp.concatenate([lax.slice_in_dim(block, 1, length, axis=axis_pos), zero_slab], axis_pos)

def per_device(rows):
    return rows.reshape(rows.shape[0], DEVICES, VOX_DEV).transpose(1, 0, 2)

def reference(features, grad_out, weights, neighbor_map, send_list):
    channels = features.shape[0]
    feat_dev = per_device(features)
    grad_dev = per_device(grad_out)
    map_dev = per_device(neighbor_map)
    sends = send_list.reshape(DEVICES, HALO)
    zero_column = jnp.zeros((DEVICES, channels, 1), grad_out.dtype)
    padded = jnp.concatenate([grad_dev, zero_column], axis=2)
    outgoing = jax.vmap(lambda block, indices: jnp.take(block, indices, axis=1))(padded, sends)
    grid = outgoing.reshape(N_GX, N_GY, N_GZ, channels, HALO)
    pieces = []
    start_col = 0
    for stencil_displacement, place_room_limit in zip(transfer_headings(), block_room_limits()):
        piece = grid[..., start_col:start_col + place_room_limit]
        for axis_pos in range(3):
            if stencil_displacement[axis_pos] != 0:
                piece = shifted(piece, axis_pos, stencil_displacement[axis_pos])
        pieces.append(piece)
        start_col += place_room_limit
    halo_all = jnp.concatenate(pieces, axis=4).reshape(DEVICES, channels, HALO)
    lookup = jnp.concatenate([grad_dev, halo_all, zero_column], axis=2)
    weights_wide = weights.astype(jnp.float32)

    def one_device(inputs):
        table_one, feat_one, map_one = inputs
        feat_wide = feat_one.astype(jnp.float32)

        def accumulate(running, parts):
            kernel, indices = parts
            picked = jnp.take(table_one, indices, axis=1).astype(jnp.float32)
            running = running + jnp.dot(kernel, picked, precision=lax.Precision.HIGHEST)
            partial_w = jnp.dot(feat_wide, picked.T, precision=lax.Precision.HIGHEST)
            return (running, partial_w)
        running, incomplete_totals = lax.scan(accumulate, jnp.zeros((channels, VOX_DEV), jnp.float32), (weights_wide, map_one))
        return (running.astype(jnp.bfloat16), incomplete_totals)
    grads_dev, partial_dev = lax.map(one_device, (lookup, feat_dev, map_dev))
    grad_in = grads_dev.transpose(1, 0, 2).reshape(channels, DEVICES * VOX_DEV)
    grad_weights = lax.optimization_barrier(jnp.sum(partial_dev, axis=0)) * (1.0 / math.sqrt(VOX_DEV * DEVICES))
    return (grad_in, grad_weights)
```

```python
import functools
import math

import jax
import jax.numpy as jnp
import numpy as np
from jax import lax
from jax.experimental import pallas as pl
from jax.experimental.pallas import tpu as pltpu
from jax.sharding import PartitionSpec as P

MESH = pl.DeviceIdType.MESH
AXES = ("gx", "gy", "gz")
KVOL = 27
MIDDLE = KVOL // 2
OTHERS = [k for k in range(KVOL) if k != MIDDLE]
PAIRS = len(OTHERS) // 2
TILES = 128
ROWS_MM = 2048
ROWS_BODY = 512

DIRECTIONS = [
    d
    for weight in (1, 2, 3)
    for d in [(x, y, z) for x in (-1, 0, 1) for y in (-1, 0, 1) for z in (-1, 0, 1)]
    if sum(map(abs, d)) == weight
]
CAPS = [512 if sum(map(abs, d)) == 1 else 128 for d in DIRECTIONS]
STARTS = [sum(CAPS[:j]) for j in range(len(CAPS))]
HALO = sum(CAPS)

NT = (((1,), (1,)), ((), ()))


def lane_is_low(rows):
    return lax.broadcasted_iota(jnp.int32, (rows, 128), 1) < 64


def row_masks():
    sub = lax.broadcasted_iota(jnp.int32, (8, 128), 0)
    return [sub == r for r in range(8)]


def gather_pair(table, view, consts, masks, low):
    found = [None, None]
    for q in range(4):
        here = view.at[pl.ds(q * 2, view.shape[0] - 6)]
        for side in range(2):
            for r in range(2):
                row = table[pl.ds(here[consts[side * 2 + r]], 8, stride=0), :]
                first = q == 0 and r == 0
                found[side] = (
                    row if first else jnp.where(masks[q * 2 + r], row, found[side])
                )
    return jnp.where(low, found[0], found[1])


def exchange_kernel(sizes, consts, sends, grad, table, out_rows, in_rows, send_sem, recv_sem):
    slots = grad.shape[1]
    me = [lax.axis_index(a) for a in AXES]

    def inside(sign, d):
        ok = None
        for axis in range(3):
            if d[axis] != 0:
                there = me[axis] + sign * d[axis]
                here = (there >= 0) & (there < sizes[axis])
                ok = here if ok is None else ok & here
        return ok

    def device(d):
        return tuple(me[axis] + d[axis] for axis in range(3))

    in_rows[...] = jnp.zeros_like(in_rows)
    barrier = pltpu.get_barrier_semaphore()
    for d in DIRECTIONS:

        @pl.when(inside(1, d))
        def _(d=d):
            pl.semaphore_signal(barrier, inc=1, device_id=device(d), device_id_type=MESH)

    low8, low64, masks = lane_is_low(8), lane_is_low(64), row_masks()
    one, zero = consts[1], consts[0]

    def transpose_step(b, carry):
        cols = pl.ds(pl.multiple_of(b * 128, 128), 128)
        block = grad[:, cols].astype(jnp.float32)
        table[cols, :] = jnp.concatenate([block, block], 0).T
        return carry

    lax.fori_loop(0, slots // 128, transpose_step, 0)
    table[slots : slots + 8, :] = jnp.zeros((8, 128), jnp.float32)

    def gather_unit(src, half, dst):
        cs = [zero, one, zero + half, one + half]
        view = sends.at[pl.ds(src, half + 64)]
        for t in range(4):
            parts = [
                gather_pair(table, view.at[pl.ds(t * 16 + h * 8, half + 8)], cs, masks, low8)
                for h in range(2)
            ]
            out_rows[pl.ds(pl.multiple_of(dst + t * 16, 16), 16), :] = jnp.concatenate(
                parts, 0
            ).astype(jnp.bfloat16)

    def face_unit(i, carry):
        gather_unit((i // 4) * 512 + (i % 4) * 64, 256, i * 64)
        return carry

    def edge_unit(i, carry):
        gather_unit(3072 + i * 128, 64, 1536 + i * 64)
        return carry

    def copy(j):
        rows = pl.ds(STARTS[j] // 2, CAPS[j] // 2)
        return pltpu.make_async_remote_copy(
            src_ref=out_rows.at[rows],
            dst_ref=in_rows.at[rows],
            send_sem=send_sem.at[j],
            recv_sem=recv_sem.at[j],
            device_id=device(DIRECTIONS[j]),
            device_id_type=MESH,
        )

    lax.fori_loop(0, 24, face_unit, 0)
    around = 1
    for axis in range(3):
        around *= 1 + (me[axis] > 0).astype(jnp.int32) + (me[axis] < sizes[axis] - 1).astype(jnp.int32)
    pl.semaphore_wait(barrier, around - 1)

    for j in range(6):

        @pl.when(inside(1, DIRECTIONS[j]))
        def _(j=j):
            copy(j).start()

    lax.fori_loop(0, 20, edge_unit, 0)
    for j in range(6, 26):

        @pl.when(inside(1, DIRECTIONS[j]))
        def _(j=j):
            copy(j).start()

    for j in range(26):

        @pl.when(inside(-1, DIRECTIONS[j]))
        def _(j=j):
            copy(j).wait_recv()

    def spread(src, dst, half):
        x = in_rows[pl.ds(pl.multiple_of(src, 64), 64), :].astype(jnp.float32)
        turned = pltpu.roll(x, 64, 1)
        dst = pl.multiple_of(dst, 64)
        table[pl.ds(dst, 64), :] = jnp.where(low64, x, turned)
        table[pl.ds(dst + half, 64), :] = jnp.where(low64, turned, x)

    def face_spread(i, carry):
        spread(i * 64, slots + (i // 4) * 512 + (i % 4) * 64, 256)
        return carry

    def edge_spread(i, carry):
        spread(1536 + i * 64, slots + 3072 + i * 128, 64)
        return carry

    lax.fori_loop(0, 24, face_spread, 0)
    lax.fori_loop(0, 20, edge_spread, 0)
    rest = table.shape[0] - slots - HALO
    table[slots + HALO :, :] = jnp.zeros((rest, 128), jnp.float32)

    for j in range(26):

        @pl.when(inside(1, DIRECTIONS[j]))
        def _(j=j):
            copy(j).wait_send()


def conv_kernel(consts, maps, table, grad, features, pair_weights, mid_weights, mid_map, grad_in, grad_w, total, picked):
    slots = grad.shape[1]
    p = pl.program_id(0)
    low, masks = lane_is_low(8), row_masks()
    cs = [consts[0], consts[1], consts[0] + slots, consts[1] + slots]

    @pl.when(p == 0)
    def _():
        grad_w[...] = jnp.zeros_like(grad_w)

        def middle(i, carry):
            cols = pl.ds(pl.multiple_of(i * 512, 512), 512)
            used = mid_map[:, cols] < slots
            g = jnp.where(used, grad[:, cols].astype(jnp.float32), 0.0).astype(jnp.bfloat16)
            total[:, cols] = jnp.dot(mid_weights[...], g, preferred_element_type=jnp.float32)
            grad_w[PAIRS, :, 0:64] += lax.dot_general(
                features[:, cols], g, NT, preferred_element_type=jnp.float32
            )
            return carry

        lax.fori_loop(0, slots // 512, middle, 0)

    def gather_step(j, carry):
        row = pl.multiple_of(j * ROWS_BODY, ROWS_BODY)
        view = maps.at[pl.ds(row, slots + ROWS_BODY)]
        for t in range(ROWS_BODY // 16):
            parts = [
                gather_pair(table, view.at[pl.ds(t * 16 + h * 8, slots + 8)], cs, masks, low)
                for h in range(2)
            ]
            picked[pl.ds(row + t * 16, 16), :] = jnp.concatenate(parts, 0).astype(jnp.bfloat16)
        return carry

    lax.fori_loop(0, slots // ROWS_BODY, gather_step, 0)

    def matmul_step(i, carry):
        cols = pl.ds(pl.multiple_of(i * ROWS_MM, ROWS_MM), ROWS_MM)
        rows = picked[cols, :]
        grad_w[p] += jnp.dot(features[:, cols], rows, preferred_element_type=jnp.float32)
        total[:, cols] += lax.dot_general(
            pair_weights[p], rows, NT, preferred_element_type=jnp.float32
        )
        return carry

    lax.fori_loop(0, slots // ROWS_MM, matmul_step, 0)

    @pl.when(p == PAIRS - 1)
    def _():
        def finish(i, carry):
            cols = pl.ds(pl.multiple_of(i * 512, 512), 512)
            grad_in[:, cols] = total[:, cols].astype(jnp.bfloat16)
            return carry

        lax.fori_loop(0, slots // 512, finish, 0)


def reduce_kernel(sizes, scale, terms, out, half, from_pair, from_y, from_x, back_y, whole, part, send, recv):
    nx, ny, _ = sizes
    x, y, z = [lax.axis_index(a) for a in AXES]
    own = TILES // 2
    share = own // ny

    peers_y = [lax.rem(y + s, ny) for s in range(1, ny)]
    peers_x = [lax.rem(x + s, nx) for s in range(1, nx)]
    barrier = pltpu.get_barrier_semaphore()
    targets = [(x, y, 1 - z)] + [(x, q, z) for q in peers_y] + [(q, y, z) for q in peers_x]
    for target in targets:
        pl.semaphore_signal(barrier, inc=1, device_id=target, device_id_type=MESH)
    pl.semaphore_wait(barrier, len(targets))

    def copy(src, dst, slot_send, slot_recv, target):
        return pltpu.make_async_remote_copy(
            src_ref=src,
            dst_ref=dst,
            send_sem=send.at[slot_send],
            recv_sem=recv.at[slot_recv],
            device_id=target,
            device_id_type=MESH,
        )

    first = copy(terms.at[pl.ds((1 - z) * own, own)], from_pair, 0, 0, (x, y, 1 - z))
    first.start()
    first.wait()
    half[...] = terms[pl.ds(z * own, own)] + from_pair[...]

    def to_all(base, peers, source, landing, me, place):
        sent = []
        for s, q in enumerate(peers):
            c = copy(source(q), landing(me), base + s, base + s, place(q))
            c.start()
            sent.append(c)
        return sent

    base_y = 1
    sent = to_all(
        base_y,
        peers_y,
        lambda q: half.at[pl.ds(q * share, share)],
        lambda me: from_y.at[me],
        y,
        lambda q: (x, q, z),
    )
    from_y[y] = half[pl.ds(y * share, share)]
    for c in sent:
        c.wait()
    acc = from_y[0]
    for s in range(1, ny):
        acc = acc + from_y[s]
    part[...] = acc

    base_x = base_y + ny - 1
    sent = to_all(
        base_x, peers_x, lambda q: part, lambda me: from_x.at[me], x, lambda q: (q, y, z)
    )
    from_x[x] = part[...]
    for c in sent:
        c.wait()
    acc = from_x[0]
    for s in range(1, nx):
        acc = acc + from_x[s]
    back_y[pl.ds(y * share, share)] = acc * scale

    base_b = base_x + nx - 1
    mine = back_y.at[pl.ds(y * share, share)]
    sent = to_all(base_b, peers_y, lambda q: mine, lambda me: mine, y, lambda q: (x, q, z))
    for c in sent:
        c.wait()
    last = base_b + ny - 1
    final = copy(back_y, whole.at[pl.ds(z * own, own)], last, last, (x, y, 1 - z))
    final.start()
    whole[pl.ds(z * own, own)] = back_y[...]
    final.wait()

    per = 8
    for i in range(PAIRS):
        block = whole[i * per : (i + 1) * per].reshape(64, 128)
        out[OTHERS[2 * i]] = block[:, :64]
        out[OTHERS[2 * i + 1]] = block[:, 64:]
    out[MIDDLE] = whole[PAIRS * per : (PAIRS + 1) * per].reshape(64, 128)[:, :64]


def solution(mesh):
    sizes = tuple(mesh.shape[a] for a in AXES)
    nx, ny, nz = sizes
    vmem = pl.BlockSpec(memory_space=pltpu.VMEM)
    smem = pl.BlockSpec(memory_space=pltpu.SMEM)

    def per_device(features, grad_out, weights, neighbor_map, send_list):
        slots = grad_out.shape[1]
        rows = slots + HALO + 16
        consts = jnp.arange(8, dtype=jnp.int32)
        table = pl.pallas_call(
            functools.partial(exchange_kernel, sizes),
            in_specs=[smem, smem, vmem],
            out_specs=vmem,
            out_shape=jax.ShapeDtypeStruct((rows, 128), jnp.float32),
            scratch_shapes=[
                pltpu.VMEM((HALO // 2, 128), jnp.bfloat16),
                pltpu.VMEM((HALO // 2, 128), jnp.bfloat16),
                pltpu.SemaphoreType.DMA((26,)),
                pltpu.SemaphoreType.DMA((26,)),
            ],
            compiler_params=pltpu.CompilerParams(
                collective_id=0, has_side_effects=True, vmem_limit_bytes=32 * 2**20
            ),
            name="exchange",
        )(consts, send_list, grad_out)

        maps = jnp.concatenate([neighbor_map[:MIDDLE], neighbor_map[MIDDLE + 1 :]], 0)
        others = jnp.concatenate([weights[:MIDDLE], weights[MIDDLE + 1 :]], 0)
        pair_weights = others.reshape(PAIRS, 2, 64, 64).transpose(0, 2, 1, 3).reshape(PAIRS, 64, 128)
        grad_in, terms = pl.pallas_call(
            conv_kernel,
            grid=(PAIRS,),
            in_specs=[smem, pl.BlockSpec((2 * slots,), lambda i: (i,), memory_space=pltpu.SMEM)]
            + [vmem] * 6,
            out_specs=[vmem, vmem],
            out_shape=[
                jax.ShapeDtypeStruct((64, slots), jnp.bfloat16),
                jax.ShapeDtypeStruct((TILES // 8, 64, 128), jnp.float32),
            ],
            scratch_shapes=[
                pltpu.VMEM((64, slots), jnp.float32),
                pltpu.VMEM((slots, 128), jnp.bfloat16),
            ],
            compiler_params=pltpu.CompilerParams(vmem_limit_bytes=40 * 2**20),
            name="conv",
        )(
            consts,
            maps.reshape(-1),
            table,
            grad_out,
            features,
            pair_weights,
            weights[MIDDLE],
            neighbor_map[MIDDLE : MIDDLE + 1],
        )

        own = TILES // 2
        share = own // ny
        copies = 2 + 2 * (ny - 1) + nx - 1
        tile = (8, 128)
        grad_weights = pl.pallas_call(
            functools.partial(reduce_kernel, sizes, 1.0 / math.sqrt(slots * nx * ny * nz)),
            in_specs=[vmem],
            out_specs=vmem,
            out_shape=jax.ShapeDtypeStruct((KVOL, 64, 64), jnp.float32),
            scratch_shapes=[
                pltpu.VMEM((own,) + tile, jnp.float32),
                pltpu.VMEM((own,) + tile, jnp.float32),
                pltpu.VMEM((ny, share) + tile, jnp.float32),
                pltpu.VMEM((nx, share) + tile, jnp.float32),
                pltpu.VMEM((own,) + tile, jnp.float32),
                pltpu.VMEM((TILES,) + tile, jnp.float32),
                pltpu.VMEM((share,) + tile, jnp.float32),
                pltpu.SemaphoreType.DMA((copies,)),
                pltpu.SemaphoreType.DMA((copies,)),
            ],
            compiler_params=pltpu.CompilerParams(
                collective_id=1, has_side_effects=True, vmem_limit_bytes=32 * 2**20
            ),
            name="reduce",
        )(terms.reshape((TILES,) + tile))
        return (grad_in, grad_weights)

    placed = (P(None, AXES), P(None, AXES), P(), P(None, AXES), P(AXES))
    return jax.shard_map(
        per_device,
        mesh=mesh,
        in_specs=placed,
        out_specs=(P(None, AXES), P()),
        check_vma=False,
    )
```

```python
import functools
import math

import jax
import jax.numpy as jnp
import numpy as np
from jax import lax
from jax.experimental import pallas as pl
from jax.experimental.pallas import tpu as pltpu
from jax.sharding import PartitionSpec as P

MESH = pl.DeviceIdType.MESH
AXES = ("gx", "gy", "gz")
KVOL = 27
MIDDLE = KVOL // 2
PAIRS = MIDDLE
LATE = 2
EARLY_TILES = (PAIRS - LATE + 1) * 8
RADIX = 16
QUARTERS = 4
PIECES = (1, 8, 15, 22)
ROWS_MM = 2048
ROWS_BODY = 512

DIRECTIONS = [
    d
    for weight in (1, 2, 3)
    for d in [(x, y, z) for x in (-1, 0, 1) for y in (-1, 0, 1) for z in (-1, 0, 1)]
    if sum(map(abs, d)) == weight
]
CAPS = [512 if sum(map(abs, d)) == 1 else 128 for d in DIRECTIONS]
STARTS = [sum(CAPS[:j]) for j in range(len(CAPS))]
HALO = sum(CAPS)

NT = (((1,), (1,)), ((), ()))


def lane_is_low(rows):
    return lax.broadcasted_iota(jnp.int32, (rows, 128), 1) < 64


def row_masks():
    sub = lax.broadcasted_iota(jnp.int32, (8, 128), 0)
    return [sub == r for r in range(8)]


def gather_pair(table, pointers, at, masks, low):
    found = []
    for views in pointers:
        rows = None
        for r in range(8):
            row = table[pl.ds(views[r % 4][at + r // 4 * 4], 8, stride=0), :]
            rows = row if r == 0 else jnp.where(masks[r], row, rows)
        found.append(rows)
    return jnp.where(low, found[0], found[1])


def kernel(sizes, scale, consts, sends_in, map_a, map_b, mid_maps, grad, features_in, weights,
           grad_in, grad_w, total, staged, table, picked, whole, terms, out_rows, in_rows, halo_send, halo_recv,
           features, sends, both, early_terms, early_y, early_g, early_part, late_y, late_g, late_part,
           send, recv, load):
    slots = grad.shape[1]
    nx, ny, nz = sizes
    me = [lax.axis_index(a) for a in AXES]
    x, y, z = me
    p = pl.program_id(0)
    low, masks = lane_is_low(8), row_masks()
    shifts = [consts[r] for r in range(4)]
    mid_block = PAIRS - LATE


    def inside(sign, d):
        ok = None
        for axis in range(3):
            if d[axis] != 0:
                there = me[axis] + sign * d[axis]
                here = (there >= 0) & (there < sizes[axis])
                ok = here if ok is None else ok & here
        return ok

    def device(d):
        return tuple(me[axis] + d[axis] for axis in range(3))

    def halo_copy(j):
        rows = pl.ds(STARTS[j] // 2, CAPS[j] // 2)
        return pltpu.make_async_remote_copy(
            src_ref=out_rows.at[rows],
            dst_ref=in_rows.at[rows],
            send_sem=halo_send.at[j],
            recv_sem=halo_recv.at[j],
            device_id=device(DIRECTIONS[j]),
            device_id_type=MESH,
        )

    def transpose_step(b, carry):
        for u in range(4):
            cols = pl.ds(pl.multiple_of(b * 512 + u * 128, 128), 128)
            block = grad[:, cols].astype(jnp.float32)
            table[cols, :] = jnp.concatenate([block, block], 0).T
        return carry

    def gather_unit(src, apart, dst):
        pointers = [[sends.at[pl.ds(src + s * apart + c, 61)] for c in shifts] for s in range(2)]
        for t in range(4):
            parts = [gather_pair(table, pointers, t * 16 + h * 8, masks, low) for h in range(2)]
            out_rows[pl.ds(pl.multiple_of(dst + t * 16, 16), 16), :] = jnp.concatenate(
                parts, 0
            ).astype(jnp.bfloat16)

    def face_unit(i, carry):
        gather_unit((i // 4) * 512 + (i % 4) * 64, 256, i * 64)
        return carry

    def edge_unit(i, carry):
        gather_unit(3072 + i * 128, 64, 1536 + i * 64)
        return carry

    def middle_step(i, carry):
        cols = pl.ds(pl.multiple_of(i * 1024, 1024), 1024)
        used = mid_maps[MIDDLE % 8 : MIDDLE % 8 + 1, cols] < slots
        g = jnp.where(used, grad[:, cols].astype(jnp.float32), 0.0).astype(jnp.bfloat16)
        total[:, cols] = jnp.dot(weights[MIDDLE], g, preferred_element_type=jnp.float32)
        terms[mid_block, :, 0:64] += lax.dot_general(
            features[:, cols], g, NT, preferred_element_type=jnp.float32
        )
        return carry

    def spread(src, dst, apart):
        rows = in_rows[pl.ds(pl.multiple_of(src, 64), 64), :].astype(jnp.float32)
        turned = pltpu.roll(rows, 64, 1)
        dst = pl.multiple_of(dst, 64)
        low64 = lane_is_low(64)
        table[pl.ds(dst, 64), :] = jnp.where(low64, rows, turned)
        table[pl.ds(dst + apart, 64), :] = jnp.where(low64, turned, rows)

    def face_spread(i, carry):
        spread(i * 64, slots + (i // 4) * 512 + (i % 4) * 64, 256)
        return carry

    def edge_spread(i, carry):
        spread(1536 + i * 64, slots + 3072 + i * 128, 64)
        return carry

    digits = [y, x * nz + z]

    def member(group, q):
        return (x, q, z) if group == 0 else (q // nz, y, lax.rem(q, nz))

    def others(group):
        return [lax.rem(digits[group] + s, RADIX) for s in range(1, RADIX)]

    load_features = pltpu.make_async_copy(features_in, features, load.at[0])
    load_sends = pltpu.make_async_copy(sends_in, sends, load.at[1])
    store_in = pltpu.make_async_copy(staged, grad_in, load.at[2])

    @pl.when(p == 0)
    def _():
        load_sends.start()
        load_features.start()
        in_rows[...] = jnp.zeros_like(in_rows)
        barrier = pltpu.get_barrier_semaphore()
        for d in DIRECTIONS:

            @pl.when(inside(1, d))
            def _(d=d):
                pl.semaphore_signal(barrier, inc=1, device_id=device(d), device_id_type=MESH)

        for group in range(2):
            for q in others(group):
                pl.semaphore_signal(
                    barrier, inc=1, device_id=member(group, q), device_id_type=MESH
                )
        terms[...] = jnp.zeros_like(terms)
        picked[slots // ROWS_BODY - 1] = jnp.zeros(picked.shape[1:], picked.dtype)
        for i in range(PAIRS):
            both[i] = jnp.concatenate([weights[i], weights[i + MIDDLE + 1]], 1)

        lax.fori_loop(0, slots // 512, transpose_step, 0)
        table[slots : slots + 8, :] = jnp.zeros((8, 128), jnp.float32)
        load_sends.wait()
        lax.fori_loop(0, 24, face_unit, 0)

        around = 1
        for axis in range(3):
            around *= (
                1
                + (me[axis] > 0).astype(jnp.int32)
                + (me[axis] < sizes[axis] - 1).astype(jnp.int32)
            )
        pl.semaphore_wait(barrier, around - 1 + 2 * (RADIX - 1))

        def start(j):
            @pl.when(inside(1, DIRECTIONS[j]))
            def _():
                halo_copy(j).start()

        for j in range(6):
            start(j)
        lax.fori_loop(0, 20, edge_unit, 0)
        for j in range(6, 26):
            start(j)

        load_features.wait()
        lax.fori_loop(0, slots // 1024, middle_step, 0)

        for j in range(26):

            @pl.when(inside(-1, DIRECTIONS[j]))
            def _(j=j):
                halo_copy(j).wait_recv()

        lax.fori_loop(0, 24, face_spread, 0)
        lax.fori_loop(0, 20, edge_spread, 0)
        rest = table.shape[0] - slots - HALO
        table[slots + HALO :, :] = jnp.zeros((rest, 128), jnp.float32)

        for j in range(26):

            @pl.when(inside(1, DIRECTIONS[j]))
            def _(j=j):
                halo_copy(j).wait_send()


    terms_tiles = terms.reshape(terms.shape[0] * 8, 8, 128)

    def exchange(slot, group, source, landing):
        return [
            pltpu.make_async_remote_copy(
                src_ref=source(q),
                dst_ref=landing(digits[group]),
                send_sem=send.at[slot * (RADIX - 1) + s],
                recv_sem=recv.at[slot * (RADIX - 1) + s],
                device_id=member(group, q),
                device_id_type=MESH,
            )
            for s, q in enumerate(others(group))
        ]

    def start_all(copies):
        for c in copies:
            c.start()

    def wait_recv(copies):
        for c in copies:
            c.wait_recv()

    def wait_send(copies):
        for c in copies:
            c.wait_send()

    def added(ref):
        acc = ref[0]
        for s in range(1, RADIX):
            acc = acc + ref[s]
        return acc

    def summation(slot, source, first, base, count, in_y, in_g, part):
        mine = pl.ds(base + y * count, count)
        phases = [
            exchange(slot, 0, lambda q: source.at[pl.ds(first + q * count, count)], lambda d: in_y.at[d]),
            exchange(slot + 1, 1, lambda q: part, lambda d: in_g.at[d]),
            exchange(slot + 2, 0, lambda q: whole.at[mine], lambda d: whole.at[mine]),
        ]

        def step(n):
            if n > 0:
                wait_recv(phases[n - 1])
            if n == 0:
                start_all(phases[0])
                in_y[y] = source[pl.ds(first + y * count, count)]
            elif n == 1:
                part[...] = added(in_y)
                start_all(phases[1])
                in_g[digits[1]] = part[...]
            elif n == 2:
                whole[mine] = added(in_g) * scale
                start_all(phases[2])
            elif n == 3:
                for copies in phases:
                    wait_send(copies)

        return step

    early_step = summation(
        0, early_terms, 0, 0, EARLY_TILES // RADIX, early_y, early_g, early_part
    )
    late_step = summation(
        3, terms_tiles, EARLY_TILES, EARLY_TILES, LATE * 8 // RADIX, late_y, late_g, late_part
    )

    def reduce_step(quarter):
        for n, at in enumerate((1, 3, 6)):

            @pl.when((p - (PAIRS - 2)) * QUARTERS + quarter == at)
            def _(n=n):
                if n == 0:
                    early_terms[...] = terms_tiles[0:EARLY_TILES]
                early_step(n)


    steps = slots // ROWS_BODY

    def matmul_piece(pair, j, piece):
        count = ROWS_BODY * 2 // len(PIECES)
        first = piece // 2 * count
        cols = pl.ds(pl.multiple_of(j * ROWS_BODY + first, count), count)
        rows = picked[j, first : first + count, :]
        if piece % 2 == 0:
            block = jnp.where(pair < mid_block, pair, pair + 1)
            terms[block] += jnp.dot(features[:, cols], rows, preferred_element_type=jnp.float32)
        else:
            total[:, cols] += lax.dot_general(
                both[pair], rows, NT, preferred_element_type=jnp.float32
            )

    def gather_step(j, carry):
        before = p * steps + j - 1
        pair_before = jnp.maximum(before, 0) // steps
        step_before = lax.rem(before + steps, steps)
        row = pl.multiple_of(j * ROWS_BODY, ROWS_BODY)
        pointers = [[m.at[pl.ds(row + c, ROWS_BODY - 3)] for c in shifts] for m in (map_a, map_b)]
        for t in range(ROWS_BODY // 16):
            if t in PIECES:
                matmul_piece(pair_before, step_before, PIECES.index(t))
            parts = [gather_pair(table, pointers, t * 16 + h * 8, masks, low) for h in range(2)]
            picked[j, t * 16 : (t + 1) * 16, :] = jnp.concatenate(parts, 0).astype(jnp.bfloat16)
        return carry

    def gather_quarter(quarter, carry):
        @pl.when(p >= PAIRS - 2)
        def _():
            reduce_step(quarter)

        some = steps // QUARTERS
        return lax.fori_loop(quarter * some, (quarter + 1) * some, gather_step, carry)

    lax.fori_loop(0, QUARTERS, gather_quarter, 0)

    @pl.when(p == PAIRS - 1)
    def _():
        for piece in range(len(PIECES)):
            matmul_piece(PAIRS - 1, steps - 1, piece)

        def put(block, first, last):
            found = whole[pl.ds(block * 8, 8)].reshape(64, 128)
            if first is not None:
                grad_w[first] = found[:, :64]
            if last is not None:
                grad_w[last] = found[:, 64:]

        late_step(0)

        def finish(i, carry):
            cols = pl.ds(pl.multiple_of(i * 1024, 1024), 1024)
            staged[:, cols] = total[:, cols].astype(jnp.bfloat16)
            return carry

        lax.fori_loop(0, slots // 1024, finish, 0)
        store_in.start()
        early_step(3)
        late_step(1)
        for i in range(PAIRS - LATE):
            put(i, i, i + MIDDLE + 1)
        put(mid_block, MIDDLE, None)
        late_step(2)
        late_step(3)
        for i in range(PAIRS - LATE, PAIRS):
            put(i + 1, i, i + MIDDLE + 1)
        store_in.wait()


def solution(mesh):
    sizes = tuple(mesh.shape[a] for a in AXES)
    nx, ny, nz = sizes
    vmem = pl.BlockSpec(memory_space=pltpu.VMEM)
    smem = pl.BlockSpec(memory_space=pltpu.SMEM)

    def per_device(features, grad_out, weights, neighbor_map, send_list):
        slots = grad_out.shape[1]
        consts = jnp.arange(4, dtype=jnp.int32)
        maps = neighbor_map.reshape(-1)
        early_share = EARLY_TILES // RADIX
        late_share = LATE * 8 // RADIX
        all_tiles = EARLY_TILES + LATE * 8
        copies = 6 * (RADIX - 1)
        anywhere = pl.BlockSpec(memory_space=pl.ANY)
        f32, bf16 = jnp.float32, jnp.bfloat16

        def tiled(*lead):
            return pltpu.VMEM(lead + (8, 128), f32)

        grad_in, grad_weights = pl.pallas_call(
            functools.partial(kernel, sizes, 1.0 / math.sqrt(slots * nx * ny * nz)),
            grid=(PAIRS,),
            in_specs=[
                smem,
                anywhere,
                pl.BlockSpec((slots,), lambda i: (i,), memory_space=pltpu.SMEM),
                pl.BlockSpec((slots,), lambda i: (i + MIDDLE + 1,), memory_space=pltpu.SMEM),
                pl.BlockSpec((8, slots), lambda i: (MIDDLE // 8, 0)),
                vmem,
                anywhere,
                vmem,
            ],
            out_specs=[anywhere, vmem],
            out_shape=[
                jax.ShapeDtypeStruct((64, slots), bf16),
                jax.ShapeDtypeStruct((KVOL, 64, 64), f32),
            ],
            scratch_shapes=[
                pltpu.VMEM((64, slots), f32),
                pltpu.VMEM((64, slots), bf16),
                pltpu.VMEM((slots + HALO + 16, 128), f32),
                pltpu.VMEM((slots // ROWS_BODY, ROWS_BODY, 128), bf16),
                tiled(all_tiles),
                pltpu.VMEM((all_tiles // 8, 64, 128), f32),
                pltpu.VMEM((HALO // 2, 128), bf16),
                pltpu.VMEM((HALO // 2, 128), bf16),
                pltpu.SemaphoreType.DMA((26,)),
                pltpu.SemaphoreType.DMA((26,)),
                pltpu.VMEM((64, slots), bf16),
                pltpu.SMEM((HALO,), jnp.int32),
                pltpu.VMEM((PAIRS, 64, 128), bf16),
                tiled(EARLY_TILES),
                tiled(RADIX, early_share),
                tiled(RADIX, early_share),
                tiled(early_share),
                tiled(RADIX, late_share),
                tiled(RADIX, late_share),
                tiled(late_share),
                pltpu.SemaphoreType.DMA((copies,)),
                pltpu.SemaphoreType.DMA((copies,)),
                pltpu.SemaphoreType.DMA((3,)),
            ],
            compiler_params=pltpu.CompilerParams(
                collective_id=0, has_side_effects=True, vmem_limit_bytes=62 * 2**20
            ),
            name="conv",
        )(consts, send_list, maps, maps, neighbor_map, grad_out, features, weights)

        return (grad_in, grad_weights)

    placed = (P(None, AXES), P(None, AXES), P(), P(None, AXES), P(AXES))
    return jax.shard_map(
        per_device,
        mesh=mesh,
        in_specs=placed,
        out_specs=(P(None, AXES), P()),
        check_vma=False,
    )
```

```python
import functools
import math

import jax
import jax.numpy as jnp
import numpy as np
from jax import lax
from jax.experimental import pallas as pl
from jax.experimental.pallas import tpu as pltpu
from jax.sharding import PartitionSpec as P

MESH = pl.DeviceIdType.MESH
AXES = ("gx", "gy", "gz")
KVOL = 27
MIDDLE = KVOL // 2
PAIRS = MIDDLE
LATE = 2
EARLY_TILES = (PAIRS - LATE + 1) * 8
RADIX = 16
QUARTERS = 4
PIECES = (2, 8, 14, 20, 26, 32, 38, 44)
ROWS_MM = 2048
ROWS_BODY = 1024

DIRECTIONS = [
    d
    for weight in (1, 2, 3)
    for d in [(x, y, z) for x in (-1, 0, 1) for y in (-1, 0, 1) for z in (-1, 0, 1)]
    if sum(map(abs, d)) == weight
]
CAPS = [512 if sum(map(abs, d)) == 1 else 128 for d in DIRECTIONS]
STARTS = [sum(CAPS[:j]) for j in range(len(CAPS))]
HALO = sum(CAPS)

NT = (((1,), (1,)), ((), ()))


def lane_is_low(rows):
    return lax.broadcasted_iota(jnp.int32, (rows, 128), 1) < 64


def row_masks():
    sub = lax.broadcasted_iota(jnp.int32, (8, 128), 0)
    return [sub == r for r in range(8)]


def gather_pair(table, pointers, at, masks, low):
    found = []
    for views in pointers:
        rows = None
        for r in range(8):
            row = table[pl.ds(views[r % 4][at + r // 4 * 4], 8, stride=0), :]
            rows = row if r == 0 else jnp.where(masks[r], row, rows)
        found.append(rows)
    return jnp.where(low, found[0], found[1])


def kernel(sizes, scale, sends_in, maps, mid_maps, grad, features_in, weights,
           grad_in, grad_w, total, table, picked, whole, terms, out_rows, in_rows, halo_send, halo_recv,
           features, sends, both, early_terms, early_y, early_g, early_part, late_y, late_g, late_part,
           send, recv, load, lists):
    slots = grad.shape[1]
    nx, ny, nz = sizes
    me = [lax.axis_index(a) for a in AXES]
    x, y, z = me
    p = pl.program_id(0)
    low, masks = lane_is_low(8), row_masks()
    shifts = [(r * nx + x) // nx for r in range(4)]

    def load_list(pair, side):
        slot = lax.rem(pair, 2) * 2 + side
        return pltpu.make_async_copy(
            maps.at[pair + side * (MIDDLE + 1)],
            lists.at[pl.ds(slot * slots, slots)],
            load.at[3 + slot],
        )

    mid_block = PAIRS - LATE


    def inside(sign, d):
        ok = None
        for axis in range(3):
            if d[axis] != 0:
                there = me[axis] + sign * d[axis]
                here = (there >= 0) & (there < sizes[axis])
                ok = here if ok is None else ok & here
        return ok

    def device(d):
        return tuple(me[axis] + d[axis] for axis in range(3))

    def halo_copy(j):
        rows = pl.ds(STARTS[j] // 2, CAPS[j] // 2)
        return pltpu.make_async_remote_copy(
            src_ref=out_rows.at[rows],
            dst_ref=in_rows.at[rows],
            send_sem=halo_send.at[j],
            recv_sem=halo_recv.at[j],
            device_id=device(DIRECTIONS[j]),
            device_id_type=MESH,
        )

    def transpose_step(b, carry):
        for u in range(4):
            cols = pl.ds(pl.multiple_of(b * 512 + u * 128, 128), 128)
            block = grad[:, cols].astype(jnp.float32)
            table[cols, :] = jnp.concatenate([block, block], 0).T
        return carry

    def gather_unit(src, apart, dst):
        pointers = [[sends.at[pl.ds(src + s * apart + c, 61)] for c in shifts] for s in range(2)]
        for t in range(4):
            parts = [gather_pair(table, pointers, t * 16 + h * 8, masks, low) for h in range(2)]
            out_rows[pl.ds(pl.multiple_of(dst + t * 16, 16), 16), :] = jnp.concatenate(
                parts, 0
            ).astype(jnp.bfloat16)

    def face_unit(i, carry):
        gather_unit((i // 4) * 512 + (i % 4) * 64, 256, i * 64)
        return carry

    def edge_unit(i, carry):
        gather_unit(3072 + i * 128, 64, 1536 + i * 64)
        return carry

    def middle_step(i, carry):
        cols = pl.ds(pl.multiple_of(i * 1024, 1024), 1024)
        used = mid_maps[MIDDLE % 8 : MIDDLE % 8 + 1, cols] < slots
        g = jnp.where(used, grad[:, cols].astype(jnp.float32), 0.0).astype(jnp.bfloat16)
        total[:, cols] = jnp.dot(weights[MIDDLE], g, preferred_element_type=jnp.float32)
        terms[mid_block, :, 0:64] += lax.dot_general(
            features[:, cols], g, NT, preferred_element_type=jnp.float32
        )
        return carry

    def spread(src, dst, apart):
        rows = in_rows[pl.ds(pl.multiple_of(src, 64), 64), :].astype(jnp.float32)
        turned = pltpu.roll(rows, 64, 1)
        dst = pl.multiple_of(dst, 64)
        low64 = lane_is_low(64)
        table[pl.ds(dst, 64), :] = jnp.where(low64, rows, turned)
        table[pl.ds(dst + apart, 64), :] = jnp.where(low64, turned, rows)

    def face_spread(i, carry):
        spread(i * 64, slots + (i // 4) * 512 + (i % 4) * 64, 256)
        return carry

    def edge_spread(i, carry):
        spread(1536 + i * 64, slots + 3072 + i * 128, 64)
        return carry

    digits = [y, x * nz + z]

    def member(group, q):
        return (x, q, z) if group == 0 else (q // nz, y, lax.rem(q, nz))

    def others(group):
        return [lax.rem(digits[group] + s, RADIX) for s in range(1, RADIX)]

    load_features = pltpu.make_async_copy(features_in, features, load.at[0])
    load_sends = pltpu.make_async_copy(sends_in, sends, load.at[1])
    store_in = pltpu.make_async_copy(total, grad_in, load.at[2])

    @pl.when(p == 0)
    def _():
        load_sends.start()
        load_features.start()
        for side in range(2):
            load_list(0, side).start()
        in_rows[...] = jnp.zeros_like(in_rows)
        barrier = pltpu.get_barrier_semaphore()
        for d in DIRECTIONS:

            @pl.when(inside(1, d))
            def _(d=d):
                pl.semaphore_signal(barrier, inc=1, device_id=device(d), device_id_type=MESH)

        for group in range(2):
            for q in others(group):
                pl.semaphore_signal(
                    barrier, inc=1, device_id=member(group, q), device_id_type=MESH
                )

        lax.fori_loop(0, slots // 512, transpose_step, 0)
        table[slots : slots + 8, :] = jnp.zeros((8, 128), jnp.float32)
        def start(j):
            @pl.when(inside(1, DIRECTIONS[j]))
            def _():
                halo_copy(j).start()

        load_sends.wait()
        around = 1
        for axis in range(3):
            around *= (
                1
                + (me[axis] > 0).astype(jnp.int32)
                + (me[axis] < sizes[axis] - 1).astype(jnp.int32)
            )
        for j in range(6):
            lax.fori_loop(4 * j, 4 * j + 4, face_unit, 0)
            if j == 2:
                pl.semaphore_wait(barrier, around - 1 + 2 * (RADIX - 1))
                for k in range(2):
                    start(k)
            if j >= 2:
                start(j)
        lax.fori_loop(0, 20, edge_unit, 0)
        for j in range(6, 26):
            start(j)

        terms[...] = jnp.zeros_like(terms)
        picked[slots // ROWS_BODY - 1] = jnp.zeros(picked.shape[1:], picked.dtype)
        for i in range(PAIRS):
            both[i] = jnp.concatenate([weights[i], weights[i + MIDDLE + 1]], 1)
        load_features.wait()
        lax.fori_loop(0, slots // 1024, middle_step, 0)

        for j in range(26):

            @pl.when(inside(-1, DIRECTIONS[j]))
            def _(j=j):
                halo_copy(j).wait_recv()

        lax.fori_loop(0, 24, face_spread, 0)
        lax.fori_loop(0, 20, edge_spread, 0)
        rest = table.shape[0] - slots - HALO
        table[slots + HALO :, :] = jnp.zeros((rest, 128), jnp.float32)

        for j in range(26):

            @pl.when(inside(1, DIRECTIONS[j]))
            def _(j=j):
                halo_copy(j).wait_send()


    terms_tiles = terms.reshape(terms.shape[0] * 8, 8, 128)

    def exchange(slot, group, source, landing):
        return [
            pltpu.make_async_remote_copy(
                src_ref=source(q),
                dst_ref=landing(digits[group]),
                send_sem=send.at[slot * (RADIX - 1) + s],
                recv_sem=recv.at[slot * (RADIX - 1) + s],
                device_id=member(group, q),
                device_id_type=MESH,
            )
            for s, q in enumerate(others(group))
        ]

    def start_all(copies):
        for c in copies:
            c.start()

    def wait_recv(copies):
        for c in copies:
            c.wait_recv()

    def wait_send(copies):
        for c in copies:
            c.wait_send()

    def added(ref):
        acc = ref[0]
        for s in range(1, RADIX):
            acc = acc + ref[s]
        return acc

    def summation(slot, source, first, base, count, in_y, in_g, part):
        mine = pl.ds(base + y * count, count)
        phases = [
            exchange(slot, 0, lambda q: source.at[pl.ds(first + q * count, count)], lambda d: in_y.at[d]),
            exchange(slot + 1, 1, lambda q: part, lambda d: in_g.at[d]),
            exchange(slot + 2, 0, lambda q: whole.at[mine], lambda d: whole.at[mine]),
        ]

        def step(n):
            if n > 0:
                wait_recv(phases[n - 1])
            if n == 0:
                start_all(phases[0])
                in_y[y] = source[pl.ds(first + y * count, count)]
            elif n == 1:
                part[...] = added(in_y)
                start_all(phases[1])
                in_g[digits[1]] = part[...]
            elif n == 2:
                whole[mine] = added(in_g) * scale
                start_all(phases[2])
            elif n == 3:
                for copies in phases:
                    wait_send(copies)

        return step

    early_step = summation(
        0, early_terms, 0, 0, EARLY_TILES // RADIX, early_y, early_g, early_part
    )
    late_step = summation(
        3, terms_tiles, EARLY_TILES, EARLY_TILES, LATE * 8 // RADIX, late_y, late_g, late_part
    )

    def reduce_step(quarter):
        for n, at in enumerate((1, 3, 6)):

            @pl.when((p - (PAIRS - 2)) * QUARTERS + quarter == at)
            def _(n=n):
                if n == 0:
                    early_terms[...] = terms_tiles[0:EARLY_TILES]
                early_step(n)


    steps = slots // ROWS_BODY

    def matmul_piece(pair, j, piece):
        count = ROWS_BODY * 2 // len(PIECES)
        first = piece // 2 * count
        cols = pl.ds(pl.multiple_of(j * ROWS_BODY + first, count), count)
        rows = picked[j, first : first + count, :]
        if piece % 2 == 0:
            block = jnp.where(pair < mid_block, pair, pair + 1)
            terms[block] += jnp.dot(features[:, cols], rows, preferred_element_type=jnp.float32)
        else:
            total[:, cols] += lax.dot_general(
                both[pair], rows, NT, preferred_element_type=jnp.float32
            )

    def gather_step(j, carry):
        before = p * steps + j - 1
        pair_before = jnp.maximum(before, 0) // steps
        step_before = lax.rem(before + steps, steps)
        row = pl.multiple_of(j * ROWS_BODY, ROWS_BODY)
        slot = lax.rem(p, 2) * 2
        pointers = [
            [lists.at[pl.ds((slot + side) * slots + row + c, ROWS_BODY - 3)] for c in shifts]
            for side in range(2)
        ]
        for t in range(ROWS_BODY // 16):
            if t in PIECES:
                matmul_piece(pair_before, step_before, PIECES.index(t))
            parts = [gather_pair(table, pointers, t * 16 + h * 8, masks, low) for h in range(2)]
            picked[j, t * 16 : (t + 1) * 16, :] = jnp.concatenate(parts, 0).astype(jnp.bfloat16)
        return carry

    for side in range(2):
        load_list(p, side).wait()

    @pl.when(p < PAIRS - 1)
    def _():
        for side in range(2):
            load_list(p + 1, side).start()

    def gather_quarter(quarter, carry):
        @pl.when(p >= PAIRS - 2)
        def _():
            reduce_step(quarter)

        some = steps // QUARTERS
        return lax.fori_loop(quarter * some, (quarter + 1) * some, gather_step, carry)

    lax.fori_loop(0, QUARTERS, gather_quarter, 0)

    @pl.when(p == PAIRS - 1)
    def _():
        for piece in range(len(PIECES)):
            matmul_piece(PAIRS - 1, steps - 1, piece)

        def put(block, first, last):
            found = whole[pl.ds(block * 8, 8)].reshape(64, 128)
            if first is not None:
                grad_w[first] = found[:, :64]
            if last is not None:
                grad_w[last] = found[:, 64:]

        late_step(0)

        store_in.start()
        early_step(3)
        late_step(1)
        for i in range(PAIRS - LATE):
            put(i, i, i + MIDDLE + 1)
        put(mid_block, MIDDLE, None)
        late_step(2)
        late_step(3)
        for i in range(PAIRS - LATE, PAIRS):
            put(i + 1, i, i + MIDDLE + 1)
        store_in.wait()


def solution(mesh):
    sizes = tuple(mesh.shape[a] for a in AXES)
    nx, ny, nz = sizes
    vmem = pl.BlockSpec(memory_space=pltpu.VMEM)
    smem = pl.BlockSpec(memory_space=pltpu.SMEM)

    def per_device(features, grad_out, weights, neighbor_map, send_list):
        slots = grad_out.shape[1]
        early_share = EARLY_TILES // RADIX
        late_share = LATE * 8 // RADIX
        all_tiles = EARLY_TILES + LATE * 8
        copies = 6 * (RADIX - 1)
        anywhere = pl.BlockSpec(memory_space=pl.ANY)
        f32, bf16 = jnp.float32, jnp.bfloat16

        def tiled(*lead):
            return pltpu.VMEM(lead + (8, 128), f32)

        grad_in, grad_weights = pl.pallas_call(
            functools.partial(kernel, sizes, 1.0 / math.sqrt(slots * nx * ny * nz)),
            grid=(PAIRS,),
            in_specs=[
                anywhere,
                anywhere,
                pl.BlockSpec((8, slots), lambda i: (MIDDLE // 8, 0)),
                vmem,
                anywhere,
                vmem,
            ],
            out_specs=[anywhere, vmem],
            out_shape=[
                jax.ShapeDtypeStruct((64, slots), f32),
                jax.ShapeDtypeStruct((KVOL, 64, 64), f32),
            ],
            scratch_shapes=[
                pltpu.VMEM((64, slots), f32),
                pltpu.VMEM((slots + HALO + 16, 128), f32),
                pltpu.VMEM((slots // ROWS_BODY, ROWS_BODY, 128), bf16),
                tiled(all_tiles),
                pltpu.VMEM((all_tiles // 8, 64, 128), f32),
                pltpu.VMEM((HALO // 2, 128), bf16),
                pltpu.VMEM((HALO // 2, 128), bf16),
                pltpu.SemaphoreType.DMA((26,)),
                pltpu.SemaphoreType.DMA((26,)),
                pltpu.VMEM((64, slots), bf16),
                pltpu.SMEM((HALO,), jnp.int32),
                pltpu.VMEM((PAIRS, 64, 128), bf16),
                tiled(EARLY_TILES),
                tiled(RADIX, early_share),
                tiled(RADIX, early_share),
                tiled(early_share),
                tiled(RADIX, late_share),
                tiled(RADIX, late_share),
                tiled(late_share),
                pltpu.SemaphoreType.DMA((copies,)),
                pltpu.SemaphoreType.DMA((copies,)),
                pltpu.SemaphoreType.DMA((7,)),
                pltpu.SMEM((4 * slots,), jnp.int32),
            ],
            compiler_params=pltpu.CompilerParams(
                collective_id=0, has_side_effects=True, vmem_limit_bytes=62 * 2**20
            ),
            name="conv",
        )(send_list, neighbor_map, neighbor_map, grad_out, features, weights)

        return (grad_in.astype(bf16), grad_weights)

    placed = (P(None, AXES), P(None, AXES), P(), P(None, AXES), P(AXES))
    return jax.shard_map(
        per_device,
        mesh=mesh,
        in_specs=placed,
        out_specs=(P(None, AXES), P()),
        check_vma=False,
    )
```

```python
import functools
import math

import jax
import jax.numpy as jnp
import numpy as np
from jax import lax
from jax.experimental import pallas as pl
from jax.experimental.pallas import tpu as pltpu
from jax.sharding import PartitionSpec as P

MESH = pl.DeviceIdType.MESH
AXES = ("gx", "gy", "gz")
KVOL = 27
MIDDLE = KVOL // 2
PAIRS = MIDDLE
LATE = 4
EARLY_TILES = (PAIRS - LATE + 1) * 8
RADIX = 16
QUARTERS = 4
PIECES = (2, 8, 14, 20, 26, 32, 38, 44)
ROWS_MM = 2048
ROWS_BODY = 1024

DIRECTIONS = [
    d
    for weight in (1, 2, 3)
    for d in [(x, y, z) for x in (-1, 0, 1) for y in (-1, 0, 1) for z in (-1, 0, 1)]
    if sum(map(abs, d)) == weight
]
CAPS = [512 if sum(map(abs, d)) == 1 else 128 for d in DIRECTIONS]
STARTS = [sum(CAPS[:j]) for j in range(len(CAPS))]
HALO = sum(CAPS)

NT = (((1,), (1,)), ((), ()))


def lane_is_low(rows):
    return lax.broadcasted_iota(jnp.int32, (rows, 128), 1) < 64


def row_masks():
    sub = lax.broadcasted_iota(jnp.int32, (8, 128), 0)
    return [sub == r for r in range(8)]


def gather_pair(table, pointers, at, masks, low):
    found = []
    for views in pointers:
        rows = None
        for r in range(8):
            row = table[pl.ds(views[r % 4][at + r // 4 * 4], 8, stride=0), :]
            rows = row if r == 0 else jnp.where(masks[r], row, rows)
        found.append(rows)
    return jnp.where(low, found[0], found[1])


def kernel(sizes, scale, sends_in, maps, mid_maps, grad, features_in, weights,
           grad_in, grad_w, total, staged, table, picked, whole, terms, out_rows, in_rows, halo_send, halo_recv,
           features, sends, both, early_terms, early_y, early_g, early_part, late_y, late_g, late_part,
           send, recv, load, lists):
    slots = grad.shape[1]
    nx, ny, nz = sizes
    me = [lax.axis_index(a) for a in AXES]
    x, y, z = me
    p = pl.program_id(0)
    low, masks = lane_is_low(8), row_masks()
    shifts = [(r * nx + x) // nx for r in range(4)]

    def load_list(pair, side):
        slot = lax.rem(pair, 2) * 2 + side
        return pltpu.make_async_copy(
            maps.at[pair + side * (MIDDLE + 1)],
            lists.at[pl.ds(slot * slots, slots)],
            load.at[3 + slot],
        )

    mid_block = PAIRS - LATE


    def inside(sign, d):
        ok = None
        for axis in range(3):
            if d[axis] != 0:
                there = me[axis] + sign * d[axis]
                here = (there >= 0) & (there < sizes[axis])
                ok = here if ok is None else ok & here
        return ok

    def device(d):
        return tuple(me[axis] + d[axis] for axis in range(3))

    def halo_copy(j):
        rows = pl.ds(STARTS[j] // 2, CAPS[j] // 2)
        return pltpu.make_async_remote_copy(
            src_ref=out_rows.at[rows],
            dst_ref=in_rows.at[rows],
            send_sem=halo_send.at[j],
            recv_sem=halo_recv.at[j],
            device_id=device(DIRECTIONS[j]),
            device_id_type=MESH,
        )

    def transpose_step(b, carry):
        for u in range(4):
            cols = pl.ds(pl.multiple_of(b * 512 + u * 128, 128), 128)
            block = grad[:, cols].astype(jnp.float32)
            table[cols, :] = jnp.concatenate([block, block], 0).T
        return carry

    def gather_unit(src, apart, dst):
        pointers = [[sends.at[pl.ds(src + s * apart + c, 61)] for c in shifts] for s in range(2)]
        for t in range(4):
            parts = [gather_pair(table, pointers, t * 16 + h * 8, masks, low) for h in range(2)]
            out_rows[pl.ds(pl.multiple_of(dst + t * 16, 16), 16), :] = jnp.concatenate(
                parts, 0
            ).astype(jnp.bfloat16)

    def face_unit(i, carry):
        gather_unit((i // 4) * 512 + (i % 4) * 64, 256, i * 64)
        return carry

    def edge_unit(i, carry):
        gather_unit(3072 + i * 128, 64, 1536 + i * 64)
        return carry

    def middle_step(i, carry):
        cols = pl.ds(pl.multiple_of(i * 1024, 1024), 1024)
        used = mid_maps[MIDDLE % 8 : MIDDLE % 8 + 1, cols] < slots
        g = jnp.where(used, grad[:, cols].astype(jnp.float32), 0.0).astype(jnp.bfloat16)
        total[:, cols] = jnp.dot(weights[MIDDLE], g, preferred_element_type=jnp.float32)
        terms[mid_block, :, 0:64] += lax.dot_general(
            features[:, cols], g, NT, preferred_element_type=jnp.float32
        )
        return carry

    def spread(src, dst, apart):
        rows = in_rows[pl.ds(pl.multiple_of(src, 64), 64), :].astype(jnp.float32)
        turned = pltpu.roll(rows, 64, 1)
        dst = pl.multiple_of(dst, 64)
        low64 = lane_is_low(64)
        table[pl.ds(dst, 64), :] = jnp.where(low64, rows, turned)
        table[pl.ds(dst + apart, 64), :] = jnp.where(low64, turned, rows)

    def face_spread(i, carry):
        spread(i * 64, slots + (i // 4) * 512 + (i % 4) * 64, 256)
        return carry

    def edge_spread(i, carry):
        spread(1536 + i * 64, slots + 3072 + i * 128, 64)
        return carry

    digits = [y, x * nz + z]

    def member(group, q):
        return (x, q, z) if group == 0 else (q // nz, y, lax.rem(q, nz))

    def others(group):
        return [lax.rem(digits[group] + s, RADIX) for s in range(1, RADIX)]

    load_features = pltpu.make_async_copy(features_in, features, load.at[0])
    load_sends = pltpu.make_async_copy(sends_in, sends, load.at[1])
    store_in = pltpu.make_async_copy(staged, grad_in, load.at[2])

    @pl.when(p == 0)
    def _():
        load_sends.start()
        load_features.start()
        for side in range(2):
            load_list(0, side).start()
        in_rows[...] = jnp.zeros_like(in_rows)
        barrier = pltpu.get_barrier_semaphore()
        for d in DIRECTIONS:

            @pl.when(inside(1, d))
            def _(d=d):
                pl.semaphore_signal(barrier, inc=1, device_id=device(d), device_id_type=MESH)

        for group in range(2):
            for q in others(group):
                pl.semaphore_signal(
                    barrier, inc=1, device_id=member(group, q), device_id_type=MESH
                )

        lax.fori_loop(0, slots // 512, transpose_step, 0)
        table[slots : slots + 8, :] = jnp.zeros((8, 128), jnp.float32)
        def start(j):
            @pl.when(inside(1, DIRECTIONS[j]))
            def _():
                halo_copy(j).start()

        load_sends.wait()
        around = 1
        for axis in range(3):
            around *= (
                1
                + (me[axis] > 0).astype(jnp.int32)
                + (me[axis] < sizes[axis] - 1).astype(jnp.int32)
            )
        for j in range(6):
            lax.fori_loop(4 * j, 4 * j + 4, face_unit, 0)
            if j == 2:
                pl.semaphore_wait(barrier, around - 1 + 2 * (RADIX - 1))
                for k in range(2):
                    start(k)
            if j >= 2:
                start(j)
        lax.fori_loop(0, 20, edge_unit, 0)
        for j in range(6, 26):
            start(j)

        terms[...] = jnp.zeros_like(terms)
        picked[slots // ROWS_BODY - 1] = jnp.zeros(picked.shape[1:], picked.dtype)
        for i in range(PAIRS):
            both[i] = jnp.concatenate([weights[i], weights[i + MIDDLE + 1]], 1)
        load_features.wait()
        lax.fori_loop(0, slots // 1024, middle_step, 0)

        for j in range(26):

            @pl.when(inside(-1, DIRECTIONS[j]))
            def _(j=j):
                halo_copy(j).wait_recv()

        lax.fori_loop(0, 24, face_spread, 0)
        lax.fori_loop(0, 20, edge_spread, 0)
        rest = table.shape[0] - slots - HALO
        table[slots + HALO :, :] = jnp.zeros((rest, 128), jnp.float32)

        for j in range(26):

            @pl.when(inside(1, DIRECTIONS[j]))
            def _(j=j):
                halo_copy(j).wait_send()


    terms_tiles = terms.reshape(terms.shape[0] * 8, 8, 128)

    def exchange(slot, group, source, landing):
        return [
            pltpu.make_async_remote_copy(
                src_ref=source(q),
                dst_ref=landing(digits[group]),
                send_sem=send.at[slot * (RADIX - 1) + s],
                recv_sem=recv.at[slot * (RADIX - 1) + s],
                device_id=member(group, q),
                device_id_type=MESH,
            )
            for s, q in enumerate(others(group))
        ]

    def start_all(copies):
        for c in copies:
            c.start()

    def wait_recv(copies):
        for c in copies:
            c.wait_recv()

    def wait_send(copies):
        for c in copies:
            c.wait_send()

    def added(ref):
        acc = ref[0]
        for s in range(1, RADIX):
            acc = acc + ref[s]
        return acc

    def summation(slot, source, first, base, count, in_y, in_g, part):
        mine = pl.ds(base + y * count, count)
        phases = [
            exchange(slot, 0, lambda q: source.at[pl.ds(first + q * count, count)], lambda d: in_y.at[d]),
            exchange(slot + 1, 1, lambda q: part, lambda d: in_g.at[d]),
            exchange(slot + 2, 0, lambda q: whole.at[mine], lambda d: whole.at[mine]),
        ]

        def step(n):
            if n > 0:
                wait_recv(phases[n - 1])
            if n == 0:
                start_all(phases[0])
                in_y[y] = source[pl.ds(first + y * count, count)]
            elif n == 1:
                part[...] = added(in_y)
                start_all(phases[1])
                in_g[digits[1]] = part[...]
            elif n == 2:
                whole[mine] = added(in_g) * scale
                start_all(phases[2])
            elif n == 3:
                for copies in phases:
                    wait_send(copies)

        return step

    early_step = summation(
        0, early_terms, 0, 0, EARLY_TILES // RADIX, early_y, early_g, early_part
    )
    late_step = summation(
        3, terms_tiles, EARLY_TILES, EARLY_TILES, LATE * 8 // RADIX, late_y, late_g, late_part
    )

    def reduce_step(quarter):
        for n, at in enumerate((1, 5, 10)):

            @pl.when((p - (PAIRS - LATE)) * QUARTERS + quarter == at)
            def _(n=n):
                if n == 0:
                    early_terms[...] = terms_tiles[0:EARLY_TILES]
                early_step(n)


    steps = slots // ROWS_BODY

    def matmul_piece(pair, j, piece):
        count = ROWS_BODY * 2 // len(PIECES)
        first = piece // 2 * count
        cols = pl.ds(pl.multiple_of(j * ROWS_BODY + first, count), count)
        rows = picked[j, first : first + count, :]
        if piece % 2 == 0:
            block = jnp.where(pair < mid_block, pair, pair + 1)
            terms[block] += jnp.dot(features[:, cols], rows, preferred_element_type=jnp.float32)
        else:
            total[:, cols] += lax.dot_general(
                both[pair], rows, NT, preferred_element_type=jnp.float32
            )

    def gather_step(j, carry):
        before = p * steps + j - 1
        pair_before = jnp.maximum(before, 0) // steps
        step_before = lax.rem(before + steps, steps)
        row = pl.multiple_of(j * ROWS_BODY, ROWS_BODY)
        slot = lax.rem(p, 2) * 2
        pointers = [
            [lists.at[pl.ds((slot + side) * slots + row + c, ROWS_BODY - 3)] for c in shifts]
            for side in range(2)
        ]
        for t in range(ROWS_BODY // 16):
            if t in PIECES:
                matmul_piece(pair_before, step_before, PIECES.index(t))
            parts = [gather_pair(table, pointers, t * 16 + h * 8, masks, low) for h in range(2)]
            picked[j, t * 16 : (t + 1) * 16, :] = jnp.concatenate(parts, 0).astype(jnp.bfloat16)
        return carry

    for side in range(2):
        load_list(p, side).wait()

    @pl.when(p < PAIRS - 1)
    def _():
        for side in range(2):
            load_list(p + 1, side).start()

    def gather_quarter(quarter, carry):
        @pl.when(p >= PAIRS - LATE)
        def _():
            reduce_step(quarter)

        some = steps // QUARTERS
        return lax.fori_loop(quarter * some, (quarter + 1) * some, gather_step, carry)

    lax.fori_loop(0, QUARTERS, gather_quarter, 0)

    @pl.when(p == PAIRS - 1)
    def _():
        for piece in range(len(PIECES)):
            matmul_piece(PAIRS - 1, steps - 1, piece)

        def put(block, first, last):
            found = whole[pl.ds(block * 8, 8)].reshape(64, 128)
            if first is not None:
                grad_w[first] = found[:, :64]
            if last is not None:
                grad_w[last] = found[:, 64:]

        late_step(0)

        def finish(i, carry):
            cols = pl.ds(pl.multiple_of(i * 1024, 1024), 1024)
            staged[:, cols] = total[:, cols].astype(jnp.bfloat16)
            return carry

        lax.fori_loop(0, slots // 1024, finish, 0)
        store_in.start()
        early_step(3)
        late_step(1)
        for i in range(PAIRS - LATE):
            put(i, i, i + MIDDLE + 1)
        put(mid_block, MIDDLE, None)
        late_step(2)
        late_step(3)
        for i in range(PAIRS - LATE, PAIRS):
            put(i + 1, i, i + MIDDLE + 1)
        store_in.wait()


def solution(mesh):
    sizes = tuple(mesh.shape[a] for a in AXES)
    nx, ny, nz = sizes
    vmem = pl.BlockSpec(memory_space=pltpu.VMEM)
    smem = pl.BlockSpec(memory_space=pltpu.SMEM)

    def per_device(features, grad_out, weights, neighbor_map, send_list):
        slots = grad_out.shape[1]
        early_share = EARLY_TILES // RADIX
        late_share = LATE * 8 // RADIX
        all_tiles = EARLY_TILES + LATE * 8
        copies = 6 * (RADIX - 1)
        anywhere = pl.BlockSpec(memory_space=pl.ANY)
        f32, bf16 = jnp.float32, jnp.bfloat16

        def tiled(*lead):
            return pltpu.VMEM(lead + (8, 128), f32)

        grad_in, grad_weights = pl.pallas_call(
            functools.partial(kernel, sizes, 1.0 / math.sqrt(slots * nx * ny * nz)),
            grid=(PAIRS,),
            in_specs=[
                anywhere,
                anywhere,
                pl.BlockSpec((8, slots), lambda i: (MIDDLE // 8, 0)),
                vmem,
                anywhere,
                vmem,
            ],
            out_specs=[anywhere, vmem],
            out_shape=[
                jax.ShapeDtypeStruct((64, slots), bf16),
                jax.ShapeDtypeStruct((KVOL, 64, 64), f32),
            ],
            scratch_shapes=[
                pltpu.VMEM((64, slots), f32),
                pltpu.VMEM((64, slots), bf16),
                pltpu.VMEM((slots + HALO + 16, 128), f32),
                pltpu.VMEM((slots // ROWS_BODY, ROWS_BODY, 128), bf16),
                tiled(all_tiles),
                pltpu.VMEM((all_tiles // 8, 64, 128), f32),
                pltpu.VMEM((HALO // 2, 128), bf16),
                pltpu.VMEM((HALO // 2, 128), bf16),
                pltpu.SemaphoreType.DMA((26,)),
                pltpu.SemaphoreType.DMA((26,)),
                pltpu.VMEM((64, slots), bf16),
                pltpu.SMEM((HALO,), jnp.int32),
                pltpu.VMEM((PAIRS, 64, 128), bf16),
                tiled(EARLY_TILES),
                tiled(RADIX, early_share),
                tiled(RADIX, early_share),
                tiled(early_share),
                tiled(RADIX, late_share),
                tiled(RADIX, late_share),
                tiled(late_share),
                pltpu.SemaphoreType.DMA((copies,)),
                pltpu.SemaphoreType.DMA((copies,)),
                pltpu.SemaphoreType.DMA((7,)),
                pltpu.SMEM((4 * slots,), jnp.int32),
            ],
            compiler_params=pltpu.CompilerParams(
                collective_id=0, has_side_effects=True, vmem_limit_bytes=62 * 2**20
            ),
            name="conv",
        )(send_list, neighbor_map, neighbor_map, grad_out, features, weights)

        return (grad_in, grad_weights)

    placed = (P(None, AXES), P(None, AXES), P(), P(None, AXES), P(AXES))
    return jax.shard_map(
        per_device,
        mesh=mesh,
        in_specs=placed,
        out_specs=(P(None, AXES), P()),
        check_vma=False,
    )
```
